32 devices in a mesh: ctx: 8 (over z, y), head: 4 (over x, core).
Axes of the slice: x: 2, y: 2, z: 4, core: 2. Of those that a mesh axis runs over, the one named last changes fastest.
Arguments:
- query: bfloat16 [2048, 4096], P(('ctx', 'head')), may hold values from -64 to 64
- key: bfloat16 [2048, 512], P(('ctx', 'head')), may hold values from -6 to 6
- value: bfloat16 [2048, 512], P(('ctx', 'head')), may hold values from -6 to 6
- grad_out: bfloat16 [2048, 4096], P('ctx', 'head'), may hold values from -6 to 6
- doc_ids: int32 [16], replicated, may hold values from 0 to 5, never falling along the last dimension, each value on 1 to 4 neighbouring positions
- relay_mask: int32 [2], replicated, may hold values from 0 to 7
- drop_bits: int32 [32, 128, 4], P('head'), may hold values from -2147483648 to 2147483647
Outputs:
- out: bfloat16 [2048, 4096], P('ctx', 'head')
- grad_query: bfloat16 [2048, 4096], P(('ctx', 'head'))
- grad_key: bfloat16 [2048, 512], P(('ctx', 'head'))
- grad_value: bfloat16 [2048, 512], P(('ctx', 'head'))
The draws below stay inside these ranges and needn't reach their ends.
Inputs may be any that keep to these rules, and one draw needn't show every extreme that they name: `doc_ids`: numbers never fall; each document spans 1 to 4 blocks and one spans exactly 4.
All inputs are finite; a program needn't handle non-finite values.
Results may differ from the reference program's by a relative error of at most 0.033.
Values may be sent and summed in bfloat16 or wider, within the bound.
No kernel may reach another device: no remote copies, remote signals or barrier semaphores. Data moves between devices by JAX's collectives and lax.ppermute only.
A program may use at most 64 MiB of HBM per device.

```python
import math
import jax
import jax.numpy as jnp
import numpy as np
from jax import lax

E = 128
BLK = 128
BLK_DEV = 2
HEADS = 32
KVH = 4
SEQ = 2048
NBLK = 16
MAXDOC = 4
DOCS = 6
N_CTX = 8


def key_matrix(key):
    base_draw = jnp.clip(jax.random.normal(jax.random.fold_in(key, 11), (SEQ, KVH * E), jnp.float32), -6.0, 6.0)
    return base_draw


def draw_key(key, part):
    base_draw = key_matrix(key)
    return base_draw.astype(jnp.bfloat16)


def draw_query(key, part):
    base_draw = jnp.clip(jax.random.normal(jax.random.fold_in(key, 21), (SEQ, HEADS * E), jnp.float32), -6.0, 6.0)
    return base_draw.astype(jnp.bfloat16)


def draw_drop_bits(key, part):
    digits = jax.random.randint(key, (HEADS, BLK, BLK // 32, 32), 0, 10, dtype=jnp.int32)
    bit_values = (digits < 9).astype(jnp.int32)
    shifted = jnp.left_shift(bit_values, jnp.arange(32, dtype=jnp.int32))
    return jnp.sum(shifted, axis=-1).astype(jnp.int32)


def block_scale(key, dims, split, smallest, high):
    level, own = 1.0, jax.random.fold_in(key, 6)
    for position, shards_of in split:
        heights = jnp.exp(jax.random.uniform(jax.random.fold_in(own, position), (shards_of,), jnp.float32, smallest / len(split), high / len(split)))
        level = level * jnp.repeat(heights, dims[position] // shards_of).reshape([-1 if axis == position else 1 for axis in range(len(dims))])
    return level


def split_up(count, total, reach, slope):
    portions = [(1 << 20) // math.isqrt(standing ** slope) + 1 for standing in range(2, count + 1)]
    surplus, counts = total - reach - (count - 1), [1] * (count - 1)
    while surplus > 0:
        movable = [i for i in range(count - 1) if counts[i] < reach]
        whole, left = sum([portions[i] for i in movable]), surplus
        for i in movable:
            extra = min(reach - counts[i], max(1, left * portions[i] // whole), surplus)
            counts[i] = counts[i] + extra
            surplus = surplus - extra
    return np.array([reach] + counts)


def ragged(key, count, total, reach, lean):
    if count == 2:
        one = jax.random.randint(key, (), max(1, total - reach), min(reach, total - 1) + 1)
        return jnp.stack([one, total - one])
    lengths = jnp.asarray(split_up(count, total, reach, lean), jnp.int32)
    couples = (count - 1) // 2
    donor, taker = lengths[1:1 + 2 * couples:2], lengths[2:2 + 2 * couples:2]
    margin = jnp.minimum(donor - 1, reach - taker)
    passed = jax.random.randint(jax.random.fold_in(key, 1), (couples,), 0, 1 << 20) % (margin + 1)
    lengths = lengths.at[1:1 + 2 * couples:2].set(donor - passed).at[2:2 + 2 * couples:2].set(taker + passed)
    return lengths[jax.random.permutation(jax.random.fold_in(key, 2), count)]


def noise(stream_key, extent, deviation, limit, pieces=(), kind=jnp.bfloat16):
    values = jax.random.normal(stream_key, extent, jnp.float32) * deviation
    if len(pieces) > 0:
        values = block_scale(stream_key, extent, pieces, -0.22, 0.18) * values
    return jnp.clip(values, min=-limit, max=limit).astype(kind)


def setup_inputs(seed: int = 0) -> dict:
    key_of = jax.random.split(jax.random.key(seed), 8)
    return {
        "query": draw_query(jax.random.fold_in(key_of[7], 71), 0),
        "key": draw_key(jax.random.fold_in(key_of[7], 71), 0),
        "value": noise(key_of[2], (SEQ, KVH * E), 1.0, 6.0, ((0, 32),)),
        "grad_out": noise(key_of[3], (SEQ, HEADS * E), 1.0, 6.0, ((0, 8), (1, 4))),
        "doc_ids": jnp.searchsorted(jnp.cumsum(ragged(key_of[4], DOCS, NBLK, MAXDOC, 1)), jnp.arange(NBLK), side="right").astype(jnp.int32),
        "relay_mask": jax.random.randint(key_of[5], (BLK_DEV,), 0, N_CTX).astype(jnp.int32),
        "drop_bits": draw_drop_bits(jax.random.fold_in(key_of[7], 71), 0),
    }


drop_scale = 1.0 / 0.9

def unpack_bits(packed_words):
    shifts = jnp.arange(32, dtype=jnp.int32)
    bit_values = jnp.right_shift(packed_words[..., None], shifts) & 1
    return bit_values.reshape(packed_words.shape[:-1] + (packed_words.shape[-1] * 32,)).astype(jnp.float32)

def keep_tile(doubled, block_index):
    start_row = (block_index % BLK).astype(jnp.int32)
    table_rows = lax.dynamic_slice(doubled, (jnp.int32(0), start_row, jnp.int32(0)), (doubled.shape[0], BLK, doubled.shape[2]))
    return unpack_bits(table_rows)

def reference(query, key, value, grad_out, doc_ids, relay_mask, drop_bits):
    inv_root = 1.0 / math.sqrt(E)
    nblocks = SEQ // BLK
    window = MAXDOC * BLK
    group_size = HEADS // KVH
    blocks = jnp.arange(nblocks, dtype=jnp.int32)
    source = BLK_DEV * jnp.bitwise_xor(blocks // BLK_DEV, relay_mask[blocks % BLK_DEV]) + blocks % BLK_DEV
    grads_packed = grad_out.reshape(nblocks, BLK, HEADS * E)[source].reshape(SEQ, KVH, group_size, E)
    queries = query.reshape(SEQ, KVH, group_size, E)
    keys = key.reshape(SEQ, KVH, E)
    values = value.reshape(SEQ, KVH, E)
    doubled = jnp.concatenate([drop_bits, drop_bits], axis=1)

    def terms(query_block):
        first_block = jnp.maximum(query_block - MAXDOC + 1, 0).astype(jnp.int32)
        query_rows = lax.dynamic_slice_in_dim(queries, query_block * BLK, BLK, 0).astype(jnp.float32)
        key_window = lax.dynamic_slice_in_dim(keys, first_block * BLK, window, 0).astype(jnp.float32)
        value_window = lax.dynamic_slice_in_dim(values, first_block * BLK, window, 0).astype(jnp.float32)
        scores = jnp.einsum('qgne,kge->gnqk', query_rows, key_window) * inv_root
        query_pos = query_block * BLK + jnp.arange(BLK, dtype=jnp.int32)
        key_pos = first_block * BLK + jnp.arange(window, dtype=jnp.int32)
        key_docs = doc_ids[key_pos // BLK]
        allowed = (key_docs[None, :] == doc_ids[query_block]) & (key_pos[None, :] <= query_pos[:, None])
        masked = jnp.where(allowed, scores, -jnp.inf)
        row_max = lax.optimization_barrier(jnp.max(masked, axis=-1, keepdims=True))
        log_total = row_max + jnp.log(lax.optimization_barrier(jnp.sum(jnp.exp(masked - row_max), axis=-1, keepdims=True)))
        probabilities = jnp.where(allowed, jnp.exp(scores - log_total), 0.0)
        keep_bits = jax.vmap(lambda offset: keep_tile(doubled, first_block + offset))(jnp.arange(MAXDOC, dtype=jnp.int32))
        keep_bits = keep_bits.transpose(1, 2, 0, 3).reshape(KVH, group_size, BLK, window)
        weights = lax.optimization_barrier((probabilities * keep_bits * drop_scale).astype(jnp.bfloat16))
        return (first_block, query_rows, key_window, value_window, probabilities, keep_bits, weights.astype(jnp.float32))

    def forward(query_block):
        first_block, query_rows, key_window, value_window, probabilities, keep_bits, weights = terms(query_block)
        result = jnp.einsum('gnqk,kge->qgne', weights, value_window)
        return result.reshape(BLK, HEADS * E).astype(jnp.bfloat16)
    out_packed = lax.map(forward, blocks)
    out_bal = out_packed[source].reshape(SEQ, HEADS * E)

    def backward(carried, query_block):
        grad_keys, grad_values = carried
        first_block, query_rows, key_window, value_window, probabilities, keep_bits, weights = terms(query_block)
        grad_rows = lax.dynamic_slice_in_dim(grads_packed, query_block * BLK, BLK, 0).astype(jnp.float32)
        out_rows = out_packed[query_block].reshape(BLK, KVH, group_size, E).astype(jnp.float32)
        row_delta = lax.optimization_barrier(jnp.sum(grad_rows * out_rows, axis=-1)).transpose(1, 2, 0)
        dweights = jnp.einsum('qgne,kge->gnqk', grad_rows, value_window)
        dscores = (probabilities * (dweights * keep_bits * drop_scale - row_delta[..., None])).astype(jnp.bfloat16)
        dscores = lax.optimization_barrier(dscores).astype(jnp.float32)
        query_grad = (inv_root * jnp.einsum('gnqk,kge->qgne', dscores, key_window)).reshape(BLK, HEADS * E).astype(jnp.bfloat16)
        key_grad = inv_root * jnp.einsum('gnqk,qgne->kge', dscores, query_rows)
        value_grad = jnp.einsum('gnqk,qgne->kge', weights, grad_rows)
        start_row = first_block * BLK
        grad_keys = lax.dynamic_update_slice_in_dim(grad_keys, lax.dynamic_slice_in_dim(grad_keys, start_row, window, 0) + key_grad, start_row, 0)
        grad_values = lax.dynamic_update_slice_in_dim(grad_values, lax.dynamic_slice_in_dim(grad_values, start_row, window, 0) + value_grad, start_row, 0)
        return ((grad_keys, grad_values), query_grad)
    initial = (jnp.zeros((SEQ, KVH, E), jnp.float32), jnp.zeros((SEQ, KVH, E), jnp.float32))
    (grad_keys, grad_values), grad_queries = lax.scan(backward, initial, blocks)
    return (out_bal, grad_queries.reshape(SEQ, HEADS * E), grad_keys.reshape(SEQ, KVH * E).astype(jnp.bfloat16), grad_values.reshape(SEQ, KVH * E).astype(jnp.bfloat16))
```

```python
import functools
import math

import jax
import jax.numpy as jnp
from jax import lax
from jax.experimental import pallas as pl
from jax.experimental.pallas import tpu as pltpu
from jax.sharding import PartitionSpec as P

E = 128
BLK = 128
WORD = 32

DOC_SHARE = 4

KEEP_RATE = 0.9
NEG = -1e30
INV_ROOT = 1.0 / math.sqrt(E)
LOG2 = INV_ROOT * math.log2(math.e)

MOST_BRANCHES = 8

VMEM_LIMIT = 48 * 1024 * 1024
PACK_LIMIT = 62 * 1024 * 1024

SMEM = pl.BlockSpec(memory_space=pltpu.SMEM)
VMEM = pl.BlockSpec(memory_space=pltpu.VMEM)
HBM = pl.BlockSpec(memory_space=pltpu.HBM)


def nt_dot(a, b):
    return lax.dot_general(a, b, (((1,), (1,)), ((), ())), preferred_element_type=jnp.float32)


def nn_dot(a, b):
    return lax.dot_general(a, b, (((1,), (0,)), ((), ())), preferred_element_type=jnp.float32)


def tn_dot(a, b):
    return lax.dot_general(a, b, (((0,), (0,)), ((), ())), preferred_element_type=jnp.float32)


def kernel_call(body, outs, specs, scratch=(), flops=0, touched=1 << 20):
    return pl.pallas_call(
        body,
        out_shape=outs,
        in_specs=specs,
        out_specs=jax.tree.map(lambda _: VMEM, outs),
        scratch_shapes=list(scratch),
        compiler_params=pltpu.CompilerParams(vmem_limit_bytes=VMEM_LIMIT),
        cost_estimate=pl.CostEstimate(flops=flops, bytes_accessed=touched, transcendentals=0),
    )


def bf16(*shape):
    return jax.ShapeDtypeStruct(shape, jnp.bfloat16)


def pack_kernel(place_ref, query_ref, key_ref, value_ref, grad_ref, *refs, count, slots):
    *out_refs, sems = refs
    piece_refs, grad_refs = out_refs[:count], out_refs[count:]
    width = query_ref.shape[1] // count
    copies = []
    for m in range(count):
        group = place_ref[1] ^ m
        columns = pl.ds(pl.multiple_of(group * E, E), E)
        copies.append((key_ref.at[:, columns], piece_refs[m].at[:, 0:E]))
        copies.append((value_ref.at[:, columns], piece_refs[m].at[:, E : 2 * E]))
        columns = pl.ds(pl.multiple_of(group * width, E), width)
        copies.append((query_ref.at[:, columns], piece_refs[m].at[:, 2 * E :]))
    for slot in range(slots):
        copies.append((grad_ref.at[slot * BLK : (slot + 1) * BLK, :], grad_refs[slot]))
    started = [pltpu.make_async_copy(*pair, sems.at[i]) for i, pair in enumerate(copies)]
    for copy in started:
        copy.start()
    for copy in started:
        copy.wait()


def pack(place, query, key, value, grad, count):
    tokens, slots = key.shape[0], grad.shape[0] // BLK
    outs = [bf16(tokens, 2 * E + query.shape[1] // count)] * count + [bf16(BLK, grad.shape[1])] * slots
    pieces = pl.pallas_call(
        functools.partial(pack_kernel, count=count, slots=slots),
        out_shape=outs,
        in_specs=[SMEM, HBM, HBM, HBM, HBM],
        out_specs=[VMEM] * len(outs),
        scratch_shapes=[pltpu.SemaphoreType.DMA((3 * count + slots,))],
        compiler_params=pltpu.CompilerParams(vmem_limit_bytes=PACK_LIMIT),
    )(place, query, key, value, grad)
    return pieces[:count], pieces[count:]


def join_kernel(place_ref, *refs, count):
    piece_refs, (out_ref, *tail_refs) = refs[:count], refs[count:]
    tokens = piece_refs[0].shape[0]
    for m, piece in enumerate(piece_refs):
        start = pl.multiple_of((place_ref[1] ^ m) * tokens, tokens)
        out_ref[pl.ds(start, tokens), :] = piece[:, 0 : 2 * E]
    for tail in tail_refs:
        tail[...] = out_ref[out_ref.shape[0] - tail.shape[0] :, :]


def join(place, pieces, lengths):
    rows, count = pieces[0].shape[0] * len(pieces), len(pieces)
    return kernel_call(
        functools.partial(join_kernel, count=count),
        [bf16(rows, 2 * E)] + [bf16(length, 2 * E) for length in lengths],
        [SMEM] + [VMEM] * count,
    )(place, *pieces)


def unpack_kernel(place_ref, *refs):
    count = (len(refs) - 3) // 2
    me = place_ref[1]
    query_ref, key_ref, value_ref = refs[2 * count :]
    width = query_ref.shape[1] // count
    for m in range(count):
        group = me ^ m
        query_ref[:, pl.ds(pl.multiple_of(group * width, E), width)] = refs[m][...]
        columns = pl.ds(pl.multiple_of(group * E, E), E)
        key_ref[:, columns] = refs[count + m][:, 0:E]
        value_ref[:, columns] = refs[count + m][:, E : 2 * E]


def unpack(place, query_pieces, kv_pieces):
    count = len(query_pieces)
    tokens, width = query_pieces[0].shape
    outs = [bf16(tokens, count * width), bf16(tokens, count * E), bf16(tokens, count * E)]
    return kernel_call(unpack_kernel, outs, [SMEM] + [VMEM] * (2 * count))(
        place, *query_pieces, *kv_pieces
    )


def combine_kernel(place_ref, own_ref, *refs, backs, count):
    back_refs, out_refs = refs[:backs], refs[backs:]
    rows = own_ref.shape[0]
    tokens = rows // count
    total = own_ref[...]
    for back in back_refs:
        term = back[...].astype(jnp.float32)
        if term.shape[0] < rows:
            term = jnp.concatenate([jnp.zeros((rows - term.shape[0], term.shape[1]), jnp.float32), term], 0)
        total = total + term
    own_ref[...] = total
    for m in range(count):
        start = pl.multiple_of((place_ref[1] ^ m) * tokens, tokens)
        out_refs[m][...] = own_ref[pl.ds(start, tokens), :].astype(jnp.bfloat16)


def combine(place, own, backs, count):
    rows, width = own.shape

    def body(place_ref, own_ref, *refs):
        *refs, total_ref = refs
        total_ref[...] = own_ref[...]
        combine_kernel(place_ref, total_ref, *refs, backs=len(backs), count=count)

    return kernel_call(
        body,
        [bf16(rows // count, width)] * count,
        [SMEM] + [VMEM] * (1 + len(backs)),
        [pltpu.VMEM(own.shape, jnp.float32)],
    )(place, own, *backs)


def keep_kernel(place_ref, bits_ref, keep_ref, *, window):
    blocks, heads = keep_ref.shape[0], keep_ref.shape[1]
    shift = lax.broadcasted_iota(jnp.int32, (WORD, BLK), 0)
    first = place_ref[0] - (window - 1)

    def head_step(h, _):
        parts = []
        for w in range(BLK // WORD):
            words = jnp.broadcast_to(bits_ref[h, w : w + 1, :], (WORD, BLK))
            parts.append((jnp.right_shift(words, shift) & 1).astype(jnp.float32))
        bits = jnp.concatenate(parts, axis=0)
        for w in range(blocks):
            keep_ref[w, h] = pltpu.roll(bits, (BLK - first - w) & (BLK - 1), axis=1)
        return 0

    lax.fori_loop(0, heads, head_step, 0)


def keep_tiles(place, drop_bits, window, blocks):
    heads = drop_bits.shape[0]
    return kernel_call(
        functools.partial(keep_kernel, window=window),
        jax.ShapeDtypeStruct((blocks, heads, BLK, BLK), jnp.float32),
        [SMEM, VMEM],
        touched=8 * blocks * heads * BLK * BLK,
    )(place, drop_bits.swapaxes(1, 2))


def attention_kernel(*refs, slots, heads, count, parts):
    place_ref, doc_ref, keep_ref = refs[:3]
    query_refs = refs[3 : 3 + count]
    part_refs = refs[3 + count : 3 + count + parts]
    grad_refs = refs[3 + count + parts : 3 + count + parts + slots]
    rest = refs[3 + count + parts + slots :]
    out_refs, rest = rest[:slots], rest[slots:]
    query_grad_refs, rest = rest[:count], rest[count:]
    own_ref, rest = rest[0], rest[1:]
    back_refs, rest = rest[: parts - 1], rest[parts - 1 :]
    query_scr, kv_scr, score_scr, dweight_scr, weight_scr, dscore_scr, sum_scr, result_scr = rest
    blocks = kv_scr.shape[0] // BLK
    window = blocks - slots + 1
    first = place_ref[0] - (window - 1)
    tokens = query_refs[0].shape[0]
    per_block = BLK // tokens

    for m in range(count):
        owner = place_ref[1] ^ m
        slot, place = owner // per_block, owner % per_block
        for h in range(heads):
            start = pl.multiple_of(slot * (heads * BLK) + h * BLK + place * tokens, tokens)
            query_scr[pl.ds(start, tokens), :] = query_refs[m][:, (h + 2) * E : (h + 3) * E]
    low = 0
    for part in part_refs:
        kv_scr[low : low + part.shape[0], :] = part[...]
        low += part.shape[0]

    for slot in range(slots):
        own = doc_ref[first + slot + window - 1]
        biases = []
        for w in range(window - 1):
            block = first + slot + w
            same = (block >= 0) & (doc_ref[jnp.maximum(block, 0)] == own)
            biases.append(jnp.where(same, 0.0, NEG).astype(jnp.float32))
        rows = slice(slot * BLK, (slot + window) * BLK)
        queries = query_scr[slot * heads * BLK : (slot + 1) * heads * BLK, :]
        grads = jnp.concatenate([grad_refs[slot][:, h * E : (h + 1) * E] for h in range(heads)], axis=0)
        keys, values = kv_scr[rows, 0:E], kv_scr[rows, E : 2 * E]
        score_scr[...] = nt_dot(keys, queries)
        dweight_scr[...] = nt_dot(values, grads)

        def head_step(h, _, slot=slot, biases=biases):
            cols = pl.ds(pl.multiple_of(h * BLK, BLK), BLK)
            causal = lax.broadcasted_iota(jnp.int32, (BLK, BLK), 0) <= lax.broadcasted_iota(
                jnp.int32, (BLK, BLK), 1
            )
            tiles = []
            for w in range(window):
                tile = score_scr[w * BLK : (w + 1) * BLK, cols]
                tiles.append(jnp.where(causal, tile, NEG) if w == window - 1 else tile + biases[w])
            top = jnp.max(functools.reduce(jnp.maximum, tiles), axis=0, keepdims=True)
            probs = [jnp.exp2((tile - top) * LOG2) for tile in tiles]
            scale = 1.0 / jnp.sum(functools.reduce(jnp.add, probs), axis=0, keepdims=True)
            delta = jnp.zeros((BLK, BLK), jnp.float32)
            kept = []
            for w in range(window):
                block = slice(w * BLK, (w + 1) * BLK)
                keep = keep_ref[slot + w, h]
                probs[w] = probs[w] * scale
                weight_scr[block, cols] = (probs[w] * keep).astype(jnp.bfloat16)
                kept.append(dweight_scr[block, cols] * keep)
                delta = delta + probs[w] * kept[w]
            delta = jnp.sum(delta, axis=0, keepdims=True)
            for w in range(window):
                dscore_scr[w * BLK : (w + 1) * BLK, cols] = (probs[w] * (kept[w] - delta)).astype(jnp.bfloat16)
            return 0

        lax.fori_loop(0, heads, head_step, 0)
        out = tn_dot(values, weight_scr[...])
        query_grad = tn_dot(keys, dscore_scr[...])
        for h in range(heads):
            cols = slice(h * BLK, (h + 1) * BLK)
            out_refs[slot][:, h * E : (h + 1) * E] = (out[:, cols].T * (1.0 / KEEP_RATE)).astype(jnp.bfloat16)
            start = (slot * heads + h) * BLK
            result_scr[start : start + BLK, :] = (query_grad[:, cols].T * (INV_ROOT / KEEP_RATE)).astype(
                jnp.bfloat16
            )
        if slot == 0:
            sum_scr[window * BLK :, :] = jnp.zeros_like(sum_scr[window * BLK :, :])
            sum_scr[rows, 0:E] = nn_dot(dscore_scr[...], queries)
            sum_scr[rows, E : 2 * E] = nn_dot(weight_scr[...], grads)
        else:
            sum_scr[rows, 0:E] += nn_dot(dscore_scr[...], queries)
            sum_scr[rows, E : 2 * E] += nn_dot(weight_scr[...], grads)

    for m in range(count):
        owner = place_ref[1] ^ m
        slot, place = owner // per_block, owner % per_block
        for h in range(heads):
            start = pl.multiple_of(slot * (heads * BLK) + h * BLK + place * tokens, tokens)
            query_grad_refs[m][:, h * E : (h + 1) * E] = result_scr[pl.ds(start, tokens), :]
    low = 0
    for target in (*back_refs, own_ref):
        rows = slice(low, low + target.shape[0])
        target[:, 0:E] = (sum_scr[rows, 0:E] * (INV_ROOT / KEEP_RATE)).astype(target.dtype)
        target[:, E : 2 * E] = (sum_scr[rows, E : 2 * E] * (1.0 / KEEP_RATE)).astype(target.dtype)
        low += target.shape[0]


def attention(place, doc_ids, keep, pieces, kv_parts, grads):
    slots, count, parts = len(grads), len(pieces), len(kv_parts)
    tokens, width = pieces[0].shape[0], grads[0].shape[1]
    heads = width // E
    blocks = sum(part.shape[0] for part in kv_parts) // BLK
    window = blocks - slots + 1
    body = functools.partial(
        attention_kernel,
        slots=slots,
        heads=heads,
        count=count,
        parts=parts,
    )
    outs = (
        [bf16(BLK, width)] * slots
        + [bf16(tokens, width)] * count
        + [jax.ShapeDtypeStruct(kv_parts[-1].shape, jnp.float32)]
        + [bf16(*part.shape) for part in kv_parts[:-1]]
    )
    results = kernel_call(
        body,
        outs,
        [SMEM, SMEM] + [VMEM] * (1 + count + parts + slots),
        [
            pltpu.VMEM((slots * heads * BLK, E), jnp.bfloat16),
            pltpu.VMEM((blocks * BLK, 2 * E), jnp.bfloat16),
            pltpu.VMEM((window * BLK, heads * BLK), jnp.float32),
            pltpu.VMEM((window * BLK, heads * BLK), jnp.float32),
            pltpu.VMEM((window * BLK, heads * BLK), jnp.bfloat16),
            pltpu.VMEM((window * BLK, heads * BLK), jnp.bfloat16),
            pltpu.VMEM((blocks * BLK, 2 * E), jnp.float32),
            pltpu.VMEM((slots * heads * BLK, E), jnp.bfloat16),
        ],
        flops=12 * slots * heads * window * BLK * BLK * E,
        touched=8 * blocks * heads * BLK * BLK,
    )(place, doc_ids, keep, *pieces, *kv_parts, *grads)
    out, results = results[:slots], results[slots:]
    query_grads, results = results[:count], results[count:]
    return out, query_grads, results[0], results[1:]


def exchange(pieces, places):
    count = len(pieces)
    return [
        lax.ppermute(piece, "head", [(i, i ^ m) for i in range(count)]) if m in places else piece
        for m, piece in enumerate(pieces)
    ]


def relay(mask, block):
    count = lax.axis_size("ctx")
    return lax.ppermute(block, "ctx", [(i, i ^ mask) for i in range(count)]) if mask else block


def by_mask(mask, step, block, *operands):
    count = lax.axis_size("ctx")
    if count <= MOST_BRANCHES:
        return lax.switch(mask, [functools.partial(step, m) for m in range(count)], block, *operands)
    block = lax.switch(mask, [functools.partial(relay, m) for m in range(count)], block)
    return step(0, block, *operands)


def on_device(query, key, value, grad_out, doc_ids, relay_mask, drop_bits):
    shards = lax.axis_size("ctx")
    count = lax.axis_size("head")
    slots = grad_out.shape[0] // BLK
    window = doc_ids.shape[0] // DOC_SHARE
    blocks = window + slots - 1
    place = jnp.stack([lax.axis_index("ctx") * slots, lax.axis_index("head")]).astype(jnp.int32)
    ahead = [(s, min(window - 1 - (s - 1) * slots, slots)) for s in range(1, -(-(window - 1) // slots) + 1)]

    def gather(mask, grad, pieces):
        grad = relay(mask, grad)
        kv, *tails = join(place, pieces, [sent * BLK for _, sent in ahead if sent < slots])
        parts = [kv]
        for s, sent in ahead:
            block = kv if sent == slots else tails.pop(0)
            parts.insert(0, lax.ppermute(block, "ctx", [(i, i + s) for i in range(shards - s)]))
        return grad, parts

    def scatter(mask, out, backs, query_grads):
        out = relay(mask, out)
        backs = [
            lax.ppermute(back, "ctx", [(i + s, i) for i in range(shards - s)])
            for (s, _), back in zip(ahead, reversed(backs))
        ]
        return out, backs, exchange(query_grads, range(2, count))

    def finish(mask, out, own, backs, query_grads):
        out = relay(mask, out)
        query_grads = exchange(query_grads, range(1, 2))
        return out, unpack(place, query_grads, exchange(combine(place, own, backs, count), range(1, count)))

    pieces, grads = pack(place, query, key, value, grad_out, count)
    pieces = exchange(pieces, range(1, count))
    keep = keep_tiles(place, drop_bits, window, blocks)
    grad_0 = by_mask(relay_mask[0], relay, grads[0])
    grad_1, parts = by_mask(relay_mask[1], gather, grads[1], pieces)
    out, query_grads, own, backs = attention(place, doc_ids, keep, pieces, parts, [grad_0, grad_1])
    out_0, backs, query_grads = by_mask(relay_mask[0], scatter, out[0], backs, query_grads)
    out_1, token_grads = by_mask(relay_mask[1], finish, out[1], own, backs, query_grads)
    return jnp.concatenate([out_0, out_1], axis=0), *token_grads


def solution(mesh):
    placed = (
        P(("ctx", "head"), None),
        P(("ctx", "head"), None),
        P(("ctx", "head"), None),
        P("ctx", "head"),
        P(),
        P(),
        P("head", None, None),
    )
    return jax.shard_map(
        on_device,
        mesh=mesh,
        in_specs=placed,
        out_specs=(
            P("ctx", "head"),
            P(("ctx", "head"), None),
            P(("ctx", "head"), None),
            P(("ctx", "head"), None),
        ),
        check_vma=False,
    )
```

```python
import functools
import math

import jax
import jax.numpy as jnp
from jax import lax
from jax.experimental import pallas as pl
from jax.experimental.pallas import tpu as pltpu
from jax.sharding import PartitionSpec as P

E = 128
BLK = 128
WORD = 32

DOC_SHARE = 4

KEEP_RATE = 0.9
NEG = -1e30
INV_ROOT = 1.0 / math.sqrt(E)
LOG2 = INV_ROOT * math.log2(math.e)

MOST_BRANCHES = 8

VMEM_LIMIT = 48 * 1024 * 1024
PACK_LIMIT = 62 * 1024 * 1024

SMEM = pl.BlockSpec(memory_space=pltpu.SMEM)
VMEM = pl.BlockSpec(memory_space=pltpu.VMEM)
HBM = pl.BlockSpec(memory_space=pltpu.HBM)


def nt_dot(a, b):
    return lax.dot_general(a, b, (((1,), (1,)), ((), ())), preferred_element_type=jnp.float32)


def nn_dot(a, b):
    return lax.dot_general(a, b, (((1,), (0,)), ((), ())), preferred_element_type=jnp.float32)


def tn_dot(a, b):
    return lax.dot_general(a, b, (((0,), (0,)), ((), ())), preferred_element_type=jnp.float32)


def kernel_call(body, outs, specs, scratch=(), flops=0, touched=1 << 20):
    return pl.pallas_call(
        body,
        out_shape=outs,
        in_specs=specs,
        out_specs=jax.tree.map(lambda _: VMEM, outs),
        scratch_shapes=list(scratch),
        compiler_params=pltpu.CompilerParams(vmem_limit_bytes=VMEM_LIMIT),
        cost_estimate=pl.CostEstimate(flops=flops, bytes_accessed=touched, transcendentals=0),
    )


def bf16(*shape):
    return jax.ShapeDtypeStruct(shape, jnp.bfloat16)


def pack_kernel(query_ref, key_ref, value_ref, grad_ref, *refs, count, slots):
    results, (sems, result_sems, *out_refs) = refs[: count + slots], refs[count + slots :]
    piece_refs, grad_refs = out_refs[:count], out_refs[count:]
    width = query_ref.shape[1] // count
    copies = []
    for m in range(count):
        group = lax.axis_index("head") ^ m
        columns = pl.ds(pl.multiple_of(group * E, E), E)
        copies.append((key_ref.at[:, columns], piece_refs[m].at[:, 0:E]))
        copies.append((value_ref.at[:, columns], piece_refs[m].at[:, E : 2 * E]))
        columns = pl.ds(pl.multiple_of(group * width, E), width)
        copies.append((query_ref.at[:, columns], piece_refs[m].at[:, 2 * E :]))
    for slot in range(slots):
        copies.append((grad_ref.at[slot * BLK : (slot + 1) * BLK, :], grad_refs[slot]))
    started = [pltpu.make_async_copy(*pair, sems.at[i]) for i, pair in enumerate(copies)]
    for copy in started:
        copy.start()
    moved = [pltpu.make_async_copy(*pair, result_sems.at[i]) for i, pair in enumerate(zip(out_refs, results))]
    for m in range(count):
        for copy in started[3 * m : 3 * m + 3]:
            copy.wait()
        moved[m].start()
    for slot in range(slots):
        started[3 * count + slot].wait()
        moved[count + slot].start()
    for copy in moved:
        copy.wait()


def pack(query, key, value, grad, count):
    tokens, slots = key.shape[0], grad.shape[0] // BLK
    outs = [bf16(tokens, 2 * E + query.shape[1] // count)] * count + [bf16(BLK, grad.shape[1])] * slots
    pieces = pl.pallas_call(
        functools.partial(pack_kernel, count=count, slots=slots),
        out_shape=outs,
        in_specs=[HBM, HBM, HBM, HBM],
        out_specs=[HBM] * len(outs),
        scratch_shapes=[pltpu.SemaphoreType.DMA((3 * count + slots,)), pltpu.SemaphoreType.DMA((count + slots,))]
        + [pltpu.VMEM(out.shape, out.dtype) for out in outs],
        compiler_params=pltpu.CompilerParams(vmem_limit_bytes=PACK_LIMIT),
    )(query, key, value, grad)
    return pieces[:count], pieces[count:]


def join_kernel(*refs, count):
    piece_refs, (out_ref, *tail_refs) = refs[:count], refs[count:]
    tokens = piece_refs[0].shape[0]
    for m, piece in enumerate(piece_refs):
        start = pl.multiple_of((lax.axis_index("head") ^ m) * tokens, tokens)
        out_ref[pl.ds(start, tokens), :] = piece[:, 0 : 2 * E]
    for tail in tail_refs:
        tail[...] = out_ref[out_ref.shape[0] - tail.shape[0] :, :]


def join(pieces, lengths):
    rows, count = pieces[0].shape[0] * len(pieces), len(pieces)
    return kernel_call(
        functools.partial(join_kernel, count=count),
        [bf16(rows, 2 * E)] + [bf16(length, 2 * E) for length in lengths],
        [VMEM] * count,
    )(*pieces)


def spread_kernel(out_ref, *refs, count):
    piece_refs, (query_ref, whole_ref, sem) = refs[:count], refs[count:]
    copy = pltpu.make_async_copy(out_ref, whole_ref.at[0:BLK, :], sem)
    copy.start()
    width = query_ref.shape[1] // count
    for m, piece in enumerate(piece_refs):
        group = lax.axis_index("head") ^ m
        query_ref[:, pl.ds(pl.multiple_of(group * width, E), width)] = piece[...]
    copy.wait()


def spread(out, query_pieces, slots):
    count = len(query_pieces)
    tokens, width = query_pieces[0].shape
    return pl.pallas_call(
        functools.partial(spread_kernel, count=count),
        out_shape=[bf16(tokens, count * width), bf16(slots * BLK, width)],
        in_specs=[VMEM] * (1 + count),
        out_specs=[VMEM, HBM],
        scratch_shapes=[pltpu.SemaphoreType.DMA],
        compiler_params=pltpu.CompilerParams(vmem_limit_bytes=VMEM_LIMIT),
    )(out, *query_pieces)


def spread_kv_kernel(after_ref, *refs, count):
    piece_refs, (key_ref, value_ref) = refs[:count], refs[count:]
    for m, piece in enumerate(piece_refs):
        columns = pl.ds(pl.multiple_of((lax.axis_index("head") ^ m) * E, E), E)
        key_ref[:, columns] = piece[:, 0:E]
        value_ref[:, columns] = piece[:, E : 2 * E]


def spread_kv(after, pieces):
    count = len(pieces)
    outs = [bf16(pieces[0].shape[0], count * E)] * 2
    return kernel_call(functools.partial(spread_kv_kernel, count=count), outs, [HBM] + [VMEM] * count)(
        after, *pieces
    )


def place_kernel(whole_ref, out_ref, placed_ref, sem, *, slot):
    copy = pltpu.make_async_copy(out_ref, placed_ref.at[slot * BLK : (slot + 1) * BLK, :], sem)
    copy.start()
    copy.wait()


def place(whole, out, slot):
    return pl.pallas_call(
        functools.partial(place_kernel, slot=slot),
        out_shape=bf16(*whole.shape),
        in_specs=[HBM, VMEM],
        out_specs=HBM,
        scratch_shapes=[pltpu.SemaphoreType.DMA],
        input_output_aliases={0: 0},
        compiler_params=pltpu.CompilerParams(vmem_limit_bytes=VMEM_LIMIT),
    )(whole, out)


def combine_kernel(own_ref, *refs, backs, count):
    back_refs, out_refs = refs[:backs], refs[backs:]
    rows = own_ref.shape[0]
    tokens = rows // count
    total = own_ref[...]
    for back in back_refs:
        term = back[...].astype(jnp.float32)
        if term.shape[0] < rows:
            term = jnp.concatenate([jnp.zeros((rows - term.shape[0], term.shape[1]), jnp.float32), term], 0)
        total = total + term
    own_ref[...] = total
    for m in range(count):
        start = pl.multiple_of((lax.axis_index("head") ^ m) * tokens, tokens)
        out_refs[m][...] = own_ref[pl.ds(start, tokens), :].astype(jnp.bfloat16)


def combine(own, backs, count):
    rows, width = own.shape

    def body(own_ref, *refs):
        *refs, total_ref = refs
        total_ref[...] = own_ref[...]
        combine_kernel(total_ref, *refs, backs=len(backs), count=count)

    return kernel_call(
        body,
        [bf16(rows // count, width)] * count,
        [VMEM] * (1 + len(backs)),
        [pltpu.VMEM(own.shape, jnp.float32)],
    )(own, *backs)


def attention_kernel(*refs, slots, heads, count, parts):
    (doc_ref, bits_ref), rest = refs[:2], refs[2:]
    query_refs, rest = rest[:count], rest[count:]
    part_refs, rest = rest[:parts], rest[parts:]
    grad_refs, rest = rest[:slots], rest[slots:]
    out_refs, rest = rest[:slots], rest[slots:]
    query_grad_refs, rest = rest[:count], rest[count:]
    own_ref, rest = rest[0], rest[1:]
    back_refs, rest = rest[: parts - 1], rest[parts - 1 :]
    query_scr, kv_scr, bits_scr, rolled_scr, weight_scr, dscore_scr, sum_scr, result_scr = rest
    blocks = kv_scr.shape[0] // BLK
    window = blocks - slots + 1
    first = lax.axis_index("ctx") * slots - (window - 1)
    tokens = query_refs[0].shape[0]
    per_block = BLK // tokens

    for m in range(count):
        owner = lax.axis_index("head") ^ m
        slot, place = owner // per_block, owner % per_block
        for h in range(heads):
            start = pl.multiple_of(slot * (heads * BLK) + h * BLK + place * tokens, tokens)
            query_scr[pl.ds(start, tokens), :] = query_refs[m][:, (h + 2) * E : (h + 3) * E]
    low = 0
    for part in part_refs:
        kv_scr[low : low + part.shape[0], :] = part[...]
        low += part.shape[0]

    words = BLK // WORD
    for h in range(heads):
        bits_scr[h * words : (h + 1) * words, :] = bits_ref[h]
    for w in range(blocks):
        rolled_scr[w] = pltpu.roll(bits_scr[...], (BLK - first - w) & (BLK - 1), axis=1)
    to_sign = WORD - 1 - lax.broadcasted_iota(jnp.int32, (WORD, BLK), 0)

    docs = doc_ref[...].astype(jnp.float32)
    numbers = lax.broadcasted_iota(jnp.int32, docs.shape, 1)
    for slot in range(slots):
        own = jnp.max(jnp.where(numbers == first + slot + window - 1, docs, NEG), axis=1, keepdims=True)
        biases = []
        for w in range(window - 1):
            document = jnp.max(jnp.where(numbers == first + slot + w, docs, NEG), axis=1, keepdims=True)
            biases.append(jnp.where(document == own, 0.0, NEG))
        rows = slice(slot * BLK, (slot + window) * BLK)
        queries = query_scr[slot * heads * BLK : (slot + 1) * heads * BLK, :]
        grads = jnp.concatenate([grad_refs[slot][:, h * E : (h + 1) * E] for h in range(heads)], axis=0)
        keys, values = kv_scr[rows, 0:E], kv_scr[rows, E : 2 * E]

        def head_step(h, _, slot=slot, biases=biases):
            cols = pl.ds(pl.multiple_of(h * BLK, BLK), BLK)
            causal = lax.broadcasted_iota(jnp.int32, (BLK, BLK), 0) <= lax.broadcasted_iota(
                jnp.int32, (BLK, BLK), 1
            )
            tiles = []
            own_queries = query_scr[pl.ds(pl.multiple_of((slot * heads + h) * BLK, BLK), BLK), :]
            scores = nt_dot(keys, own_queries)
            own_grads = grad_refs[slot][:, cols]
            dweights = nt_dot(values, own_grads)
            for w in range(window):
                tile = scores[w * BLK : (w + 1) * BLK]
                tiles.append(jnp.where(causal, tile, NEG) if w == window - 1 else tile + biases[w])
            top = jnp.max(functools.reduce(jnp.maximum, tiles), axis=0, keepdims=True)
            probs = [jnp.exp2((tile - top) * LOG2) for tile in tiles]
            scale = 1.0 / jnp.sum(functools.reduce(jnp.add, probs), axis=0, keepdims=True)
            delta = jnp.zeros((BLK, BLK), jnp.float32)
            kept = []
            for w in range(window):
                block = slice(w * BLK, (w + 1) * BLK)
                keep = [
                    jnp.left_shift(
                        jnp.broadcast_to(rolled_scr[slot + w, pl.ds(h * words + q, 1), :], (WORD, BLK)), to_sign
                    )
                    for q in range(words)
                ]
                keep = jnp.concatenate(keep, axis=0) < 0
                probs[w] = probs[w] * scale
                weight = jnp.where(keep, probs[w], 0.0)
                weight_scr[block, cols] = weight.astype(jnp.bfloat16)
                kept.append(weight * dweights[w * BLK : (w + 1) * BLK])
                delta = delta + kept[w]
            delta = jnp.sum(delta, axis=0, keepdims=True)
            for w in range(window):
                dscore_scr[w * BLK : (w + 1) * BLK, cols] = (kept[w] - probs[w] * delta).astype(jnp.bfloat16)
            return 0

        lax.fori_loop(0, heads, head_step, 0, unroll=8)
        out = tn_dot(values, weight_scr[...])
        query_grad = tn_dot(keys, dscore_scr[...])
        for h in range(heads):
            cols = slice(h * BLK, (h + 1) * BLK)
            out_refs[slot][:, h * E : (h + 1) * E] = (out[:, cols].T * (1.0 / KEEP_RATE)).astype(jnp.bfloat16)
            start = (slot * heads + h) * BLK
            result_scr[start : start + BLK, :] = (query_grad[:, cols].T * (INV_ROOT / KEEP_RATE)).astype(
                jnp.bfloat16
            )
        if slot == 0:
            sum_scr[window * BLK :, :] = jnp.zeros_like(sum_scr[window * BLK :, :])
            sum_scr[rows, 0:E] = nn_dot(dscore_scr[...], queries)
            sum_scr[rows, E : 2 * E] = nn_dot(weight_scr[...], grads)
        else:
            sum_scr[rows, 0:E] += nn_dot(dscore_scr[...], queries)
            sum_scr[rows, E : 2 * E] += nn_dot(weight_scr[...], grads)

    for m in range(count):
        owner = lax.axis_index("head") ^ m
        slot, place = owner // per_block, owner % per_block
        for h in range(heads):
            start = pl.multiple_of(slot * (heads * BLK) + h * BLK + place * tokens, tokens)
            query_grad_refs[m][:, h * E : (h + 1) * E] = result_scr[pl.ds(start, tokens), :]
    low = 0
    for target in (*back_refs, own_ref):
        rows = slice(low, low + target.shape[0])
        target[:, 0:E] = (sum_scr[rows, 0:E] * (INV_ROOT / KEEP_RATE)).astype(target.dtype)
        target[:, E : 2 * E] = (sum_scr[rows, E : 2 * E] * (1.0 / KEEP_RATE)).astype(target.dtype)
        low += target.shape[0]


def attention(doc_ids, drop_bits, pieces, kv_parts, grads):
    slots, count, parts = len(grads), len(pieces), len(kv_parts)
    tokens, width = pieces[0].shape[0], grads[0].shape[1]
    heads = width // E
    blocks = sum(part.shape[0] for part in kv_parts) // BLK
    window = blocks - slots + 1
    body = functools.partial(
        attention_kernel,
        slots=slots,
        heads=heads,
        count=count,
        parts=parts,
    )
    outs = (
        [bf16(BLK, width)] * slots
        + [bf16(tokens, width)] * count
        + [jax.ShapeDtypeStruct(kv_parts[-1].shape, jnp.float32)]
        + [bf16(*part.shape) for part in kv_parts[:-1]]
    )
    results = kernel_call(
        body,
        outs,
        [VMEM] * (2 + count + parts + slots),
        [
            pltpu.VMEM((slots * heads * BLK, E), jnp.bfloat16),
            pltpu.VMEM((blocks * BLK, 2 * E), jnp.bfloat16),
            pltpu.VMEM((heads * BLK // WORD, BLK), jnp.int32),
            pltpu.VMEM((blocks, heads * BLK // WORD, BLK), jnp.int32),
            pltpu.VMEM((window * BLK, heads * BLK), jnp.bfloat16),
            pltpu.VMEM((window * BLK, heads * BLK), jnp.bfloat16),
            pltpu.VMEM((blocks * BLK, 2 * E), jnp.float32),
            pltpu.VMEM((slots * heads * BLK, E), jnp.bfloat16),
        ],
        flops=12 * slots * heads * window * BLK * BLK * E,
    )(doc_ids.reshape(1, -1), drop_bits.swapaxes(1, 2), *pieces, *kv_parts, *grads)
    out, results = results[:slots], results[slots:]
    query_grads, results = results[:count], results[count:]
    return out, query_grads, results[0], results[1:]


def exchange(pieces, places):
    count = len(pieces)
    return [
        lax.ppermute(piece, "head", [(i, i ^ m) for i in range(count)]) if m in places else piece
        for m, piece in enumerate(pieces)
    ]


def relay(mask, block):
    count = lax.axis_size("ctx")
    return lax.ppermute(block, "ctx", [(i, i ^ mask) for i in range(count)]) if mask else block


def by_mask(mask, step, block, *operands):
    count = lax.axis_size("ctx")
    if count <= MOST_BRANCHES:
        return lax.switch(mask, [functools.partial(step, m) for m in range(count)], block, *operands)
    block = lax.switch(mask, [functools.partial(relay, m) for m in range(count)], block)
    return step(0, block, *operands)


def on_device(query, key, value, grad_out, doc_ids, relay_mask, drop_bits):
    shards = lax.axis_size("ctx")
    count = lax.axis_size("head")
    slots = grad_out.shape[0] // BLK
    window = doc_ids.shape[0] // DOC_SHARE
    ahead = [(s, min(window - 1 - (s - 1) * slots, slots)) for s in range(1, -(-(window - 1) // slots) + 1)]

    def gather(mask, grad, pieces):
        grad = relay(mask, grad)
        kv, *tails = join(pieces, [sent * BLK for _, sent in ahead if sent < slots])
        parts = [kv]
        for s, sent in ahead:
            block = kv if sent == slots else tails.pop(0)
            parts.insert(0, lax.ppermute(block, "ctx", [(i, i + s) for i in range(shards - s)]))
        return grad, parts

    def scatter(mask, out, backs, query_grads):
        out = relay(mask, out)
        backs = [
            lax.ppermute(back, "ctx", [(i + s, i) for i in range(shards - s)])
            for (s, _), back in zip(ahead, reversed(backs))
        ]
        return out, backs, exchange(query_grads, range(2, count))

    def finish(mask, out, first_out, own, backs, query_grads):
        out = relay(mask, out)
        query_grads = exchange(query_grads, range(1, 2))
        kv_grads = exchange(combine(own, backs, count), range(1, count))
        grad_q, whole = spread(first_out, query_grads, slots)
        grad_k, grad_v = spread_kv(whole, kv_grads)
        return place(whole, out, 1), grad_q, grad_k, grad_v

    pieces, grads = pack(query, key, value, grad_out, count)
    pieces = exchange(pieces, range(1, count))
    grad_0 = by_mask(relay_mask[0], relay, grads[0])
    grad_1, parts = by_mask(relay_mask[1], gather, grads[1], pieces)
    out, query_grads, own, backs = attention(doc_ids, drop_bits, pieces, parts, [grad_0, grad_1])
    out_0, backs, query_grads = by_mask(relay_mask[0], scatter, out[0], backs, query_grads)
    return by_mask(relay_mask[1], finish, out[1], out_0, own, backs, query_grads)


def solution(mesh):
    placed = (
        P(("ctx", "head"), None),
        P(("ctx", "head"), None),
        P(("ctx", "head"), None),
        P("ctx", "head"),
        P(),
        P(),
        P("head", None, None),
    )
    return jax.shard_map(
        on_device,
        mesh=mesh,
        in_specs=placed,
        out_specs=(
            P("ctx", "head"),
            P(("ctx", "head"), None),
            P(("ctx", "head"), None),
            P(("ctx", "head"), None),
        ),
        check_vma=False,
    )
```

```python
import functools
import math

import jax
import jax.numpy as jnp
from jax import lax
from jax.experimental import pallas as pl
from jax.experimental.pallas import tpu as pltpu
from jax.sharding import PartitionSpec as P

E = 128
BLK = 128
WORD = 32

DOC_SHARE = 4

KEEP_RATE = 0.9
NEG = -1e30
INV_ROOT = 1.0 / math.sqrt(E)
LOG2 = INV_ROOT * math.log2(math.e)

MOST_BRANCHES = 8

VMEM_LIMIT = 48 * 1024 * 1024
PACK_LIMIT = 62 * 1024 * 1024

SMEM = pl.BlockSpec(memory_space=pltpu.SMEM)
VMEM = pl.BlockSpec(memory_space=pltpu.VMEM)
HBM = pl.BlockSpec(memory_space=pltpu.HBM)


def nt_dot(a, b):
    return lax.dot_general(a, b, (((1,), (1,)), ((), ())), preferred_element_type=jnp.float32)


def nn_dot(a, b):
    return lax.dot_general(a, b, (((1,), (0,)), ((), ())), preferred_element_type=jnp.float32)


def tn_dot(a, b):
    return lax.dot_general(a, b, (((0,), (0,)), ((), ())), preferred_element_type=jnp.float32)


def kernel_call(body, outs, specs, scratch=(), flops=0, touched=1 << 20):
    return pl.pallas_call(
        body,
        out_shape=outs,
        in_specs=specs,
        out_specs=jax.tree.map(lambda _: VMEM, outs),
        scratch_shapes=list(scratch),
        compiler_params=pltpu.CompilerParams(vmem_limit_bytes=VMEM_LIMIT),
        cost_estimate=pl.CostEstimate(flops=flops, bytes_accessed=touched, transcendentals=0),
    )


def bf16(*shape):
    return jax.ShapeDtypeStruct(shape, jnp.bfloat16)


def pack_kernel(query_ref, key_ref, value_ref, grad_ref, *refs, count, slots):
    results, (sems, result_sems, *out_refs) = refs[: count + slots], refs[count + slots :]
    piece_refs, grad_refs = out_refs[:count], out_refs[count:]
    width = query_ref.shape[1] // count
    copies = []
    for m in range(count):
        group = lax.axis_index("head") ^ m
        columns = pl.ds(pl.multiple_of(group * E, E), E)
        copies.append((key_ref.at[:, columns], piece_refs[m].at[:, 0:E]))
        copies.append((value_ref.at[:, columns], piece_refs[m].at[:, E : 2 * E]))
        columns = pl.ds(pl.multiple_of(group * width, E), width)
        copies.append((query_ref.at[:, columns], piece_refs[m].at[:, 2 * E :]))
    for slot in range(slots):
        copies.append((grad_ref.at[slot * BLK : (slot + 1) * BLK, :], grad_refs[slot]))
    started = [pltpu.make_async_copy(*pair, sems.at[i]) for i, pair in enumerate(copies)]
    for copy in started:
        copy.start()
    moved = [pltpu.make_async_copy(*pair, result_sems.at[i]) for i, pair in enumerate(zip(out_refs, results))]
    for m in range(count):
        for copy in started[3 * m : 3 * m + 3]:
            copy.wait()
        moved[m].start()
    for slot in range(slots):
        started[3 * count + slot].wait()
        moved[count + slot].start()
    for copy in moved:
        copy.wait()


def pack(query, key, value, grad, count):
    tokens, slots = key.shape[0], grad.shape[0] // BLK
    outs = [bf16(tokens, 2 * E + query.shape[1] // count)] * count + [bf16(BLK, grad.shape[1])] * slots
    pieces = pl.pallas_call(
        functools.partial(pack_kernel, count=count, slots=slots),
        out_shape=outs,
        in_specs=[HBM, HBM, HBM, HBM],
        out_specs=[HBM] * len(outs),
        scratch_shapes=[pltpu.SemaphoreType.DMA((3 * count + slots,)), pltpu.SemaphoreType.DMA((count + slots,))]
        + [pltpu.VMEM(out.shape, out.dtype) for out in outs],
        compiler_params=pltpu.CompilerParams(vmem_limit_bytes=PACK_LIMIT),
    )(query, key, value, grad)
    return pieces[:count], pieces[count:]


def join_kernel(*refs, count):
    piece_refs, (out_ref, *tail_refs) = refs[:count], refs[count:]
    tokens = piece_refs[0].shape[0]
    for m, piece in enumerate(piece_refs):
        start = pl.multiple_of((lax.axis_index("head") ^ m) * tokens, tokens)
        out_ref[pl.ds(start, tokens), :] = piece[:, 0 : 2 * E]
    for tail in tail_refs:
        tail[...] = out_ref[out_ref.shape[0] - tail.shape[0] :, :]


def join(pieces, lengths):
    rows, count = pieces[0].shape[0] * len(pieces), len(pieces)
    return kernel_call(
        functools.partial(join_kernel, count=count),
        [bf16(rows, 2 * E)] + [bf16(length, 2 * E) for length in lengths],
        [VMEM] * count,
    )(*pieces)


def spread_kernel(out_ref, *refs, count):
    piece_refs, (far_ref, query_ref, whole_ref, sem) = refs[: count - 1], refs[count - 1 :]
    tokens = query_ref.shape[0]
    copy = pltpu.make_async_copy(out_ref, whole_ref.at[0:BLK, :], sem)
    copy.start()
    width = query_ref.shape[1] // count
    places = [m for m in range(count) if m != count // 2]
    for m, piece in zip([*places, count // 2], [*piece_refs, far_ref.at[0:tokens, :]]):
        group = lax.axis_index("head") ^ m
        query_ref[:, pl.ds(pl.multiple_of(group * width, E), width)] = piece[...]
    copy.wait()


def spread(out, pieces, far, slots):
    count = len(pieces) + 1
    tokens, width = pieces[0].shape
    return pl.pallas_call(
        functools.partial(spread_kernel, count=count),
        out_shape=[bf16(tokens, count * width), bf16(slots * BLK, width)],
        in_specs=[VMEM] * (1 + count),
        out_specs=[VMEM, HBM],
        scratch_shapes=[pltpu.SemaphoreType.DMA],
        compiler_params=pltpu.CompilerParams(vmem_limit_bytes=VMEM_LIMIT),
    )(out, *pieces, far)


def spread_kv_kernel(after_ref, *refs, count):
    piece_refs, (key_ref, value_ref) = refs[:count], refs[count:]
    for m, piece in enumerate(piece_refs):
        columns = pl.ds(pl.multiple_of((lax.axis_index("head") ^ m) * E, E), E)
        key_ref[:, columns] = piece[:, 0:E]
        value_ref[:, columns] = piece[:, E : 2 * E]


def spread_kv(after, pieces):
    count = len(pieces)
    outs = [bf16(pieces[0].shape[0], count * E)] * 2
    return kernel_call(functools.partial(spread_kv_kernel, count=count), outs, [HBM] + [VMEM] * count)(
        after, *pieces
    )


def place_kernel(whole_ref, out_ref, placed_ref, sem, *, slot):
    copy = pltpu.make_async_copy(out_ref, placed_ref.at[slot * BLK : (slot + 1) * BLK, :], sem)
    copy.start()
    copy.wait()


def place(whole, out, slot):
    return pl.pallas_call(
        functools.partial(place_kernel, slot=slot),
        out_shape=bf16(*whole.shape),
        in_specs=[HBM, VMEM],
        out_specs=HBM,
        scratch_shapes=[pltpu.SemaphoreType.DMA],
        input_output_aliases={0: 0},
        compiler_params=pltpu.CompilerParams(vmem_limit_bytes=VMEM_LIMIT),
    )(whole, out)


def combine_kernel(own_ref, *refs, backs, count):
    back_refs, out_refs = refs[:backs], refs[backs:]
    rows = own_ref.shape[0]
    tokens = rows // count
    total = own_ref[...]
    for back in back_refs:
        term = back[...].astype(jnp.float32)
        if term.shape[0] < rows:
            term = jnp.concatenate([jnp.zeros((rows - term.shape[0], term.shape[1]), jnp.float32), term], 0)
        total = total + term
    own_ref[...] = total
    for m in range(count):
        start = pl.multiple_of((lax.axis_index("head") ^ m) * tokens, tokens)
        out_refs[m][...] = own_ref[pl.ds(start, tokens), :].astype(jnp.bfloat16)


def combine(own, backs, count):
    rows, width = own.shape

    def body(own_ref, *refs):
        *refs, total_ref = refs
        total_ref[...] = own_ref[...]
        combine_kernel(total_ref, *refs, backs=len(backs), count=count)

    return kernel_call(
        body,
        [bf16(rows // count, width)] * count,
        [VMEM] * (1 + len(backs)),
        [pltpu.VMEM(own.shape, jnp.float32)],
    )(own, *backs)


def attention_kernel(*refs, slots, heads, count, parts):
    (doc_ref, bits_ref), rest = refs[:2], refs[2:]
    query_refs, rest = rest[:count], rest[count:]
    part_refs, rest = rest[:parts], rest[parts:]
    grad_refs, rest = rest[:slots], rest[slots:]
    out_refs, rest = rest[:slots], rest[slots:]
    query_grad_refs, far_ref, rest = rest[: count // 2], rest[count // 2], rest[count // 2 + 1 :]
    own_ref, rest = rest[0], rest[1:]
    back_refs, rest = rest[: parts - 1], rest[parts - 1 :]
    query_scr, kv_scr, bits_scr, rolled_scr, weight_scr, dscore_scr, sum_scr, result_scr = rest
    blocks = kv_scr.shape[0] // BLK
    window = blocks - slots + 1
    first = lax.axis_index("ctx") * slots - (window - 1)
    tokens = query_refs[0].shape[0]
    per_block = BLK // tokens

    for m in range(count):
        owner = lax.axis_index("head") ^ m
        slot, place = owner // per_block, owner % per_block
        for h in range(heads):
            start = pl.multiple_of(slot * (heads * BLK) + h * BLK + place * tokens, tokens)
            query_scr[pl.ds(start, tokens), :] = query_refs[m][:, (h + 2) * E : (h + 3) * E]
    low = 0
    for part in part_refs:
        kv_scr[low : low + part.shape[0], :] = part[...]
        low += part.shape[0]

    words = BLK // WORD
    for h in range(heads):
        bits_scr[h * words : (h + 1) * words, :] = bits_ref[h]
    for w in range(blocks):
        rolled_scr[w] = pltpu.roll(bits_scr[...], (BLK - first - w) & (BLK - 1), axis=1)
    to_sign = WORD - 1 - lax.broadcasted_iota(jnp.int32, (WORD, BLK), 0)

    docs = doc_ref[...].astype(jnp.float32)
    numbers = lax.broadcasted_iota(jnp.int32, docs.shape, 1)
    for slot in range(slots):
        own = jnp.max(jnp.where(numbers == first + slot + window - 1, docs, NEG), axis=1, keepdims=True)
        biases = []
        for w in range(window - 1):
            document = jnp.max(jnp.where(numbers == first + slot + w, docs, NEG), axis=1, keepdims=True)
            biases.append(jnp.where(document == own, 0.0, NEG))
        rows = slice(slot * BLK, (slot + window) * BLK)
        queries = query_scr[slot * heads * BLK : (slot + 1) * heads * BLK, :]
        grads = jnp.concatenate([grad_refs[slot][:, h * E : (h + 1) * E] for h in range(heads)], axis=0)
        keys, values = kv_scr[rows, 0:E], kv_scr[rows, E : 2 * E]

        def head_step(h, _, slot=slot, biases=biases):
            cols = pl.ds(pl.multiple_of(h * BLK, BLK), BLK)
            causal = lax.broadcasted_iota(jnp.int32, (BLK, BLK), 0) <= lax.broadcasted_iota(
                jnp.int32, (BLK, BLK), 1
            )
            tiles = []
            own_queries = query_scr[pl.ds(pl.multiple_of((slot * heads + h) * BLK, BLK), BLK), :]
            scores = nt_dot(keys, own_queries)
            own_grads = grad_refs[slot][:, cols]
            dweights = nt_dot(values, own_grads)
            for w in range(window):
                tile = scores[w * BLK : (w + 1) * BLK]
                tiles.append(jnp.where(causal, tile, NEG) if w == window - 1 else tile + biases[w])
            top = jnp.max(functools.reduce(jnp.maximum, tiles), axis=0, keepdims=True)
            probs = [jnp.exp2((tile - top) * LOG2) for tile in tiles]
            scale = 1.0 / jnp.sum(functools.reduce(jnp.add, probs), axis=0, keepdims=True)
            delta = jnp.zeros((BLK, BLK), jnp.float32)
            kept = []
            for w in range(window):
                block = slice(w * BLK, (w + 1) * BLK)
                keep = [
                    jnp.left_shift(
                        jnp.broadcast_to(rolled_scr[slot + w, pl.ds(h * words + q, 1), :], (WORD, BLK)), to_sign
                    )
                    for q in range(words)
                ]
                keep = jnp.concatenate(keep, axis=0) < 0
                probs[w] = probs[w] * scale
                weight = jnp.where(keep, probs[w], 0.0)
                weight_scr[block, cols] = weight.astype(jnp.bfloat16)
                kept.append(weight * dweights[w * BLK : (w + 1) * BLK])
                delta = delta + kept[w]
            delta = jnp.sum(delta, axis=0, keepdims=True)
            for w in range(window):
                dscore_scr[w * BLK : (w + 1) * BLK, cols] = (kept[w] - probs[w] * delta).astype(jnp.bfloat16)
            return 0

        lax.fori_loop(0, heads, head_step, 0, unroll=8)
        out = tn_dot(values, weight_scr[...])
        query_grad = tn_dot(keys, dscore_scr[...])
        for h in range(heads):
            cols = slice(h * BLK, (h + 1) * BLK)
            out_refs[slot][:, h * E : (h + 1) * E] = (out[:, cols].T * (1.0 / KEEP_RATE)).astype(jnp.bfloat16)
            start = (slot * heads + h) * BLK
            result_scr[start : start + BLK, :] = (query_grad[:, cols].T * (INV_ROOT / KEEP_RATE)).astype(
                jnp.bfloat16
            )
        if slot == 0:
            sum_scr[window * BLK :, :] = jnp.zeros_like(sum_scr[window * BLK :, :])
            sum_scr[rows, 0:E] = nn_dot(dscore_scr[...], queries)
            sum_scr[rows, E : 2 * E] = nn_dot(weight_scr[...], grads)
        else:
            sum_scr[rows, 0:E] += nn_dot(dscore_scr[...], queries)
            sum_scr[rows, E : 2 * E] += nn_dot(weight_scr[...], grads)

    for m in range(count):
        owner = lax.axis_index("head") ^ m
        slot, place = owner // per_block, owner % per_block
        for h in range(heads):
            start = pl.multiple_of(slot * (heads * BLK) + h * BLK + place * tokens, tokens)
            piece = result_scr[pl.ds(start, tokens), :]
            if m < count // 2:
                query_grad_refs[m][:, h * E : (h + 1) * E] = piece
            else:
                far_ref[(m - count // 2) * tokens : (m + 1 - count // 2) * tokens, h * E : (h + 1) * E] = piece
    low = 0
    for target in (*back_refs, own_ref):
        rows = slice(low, low + target.shape[0])
        target[:, 0:E] = (sum_scr[rows, 0:E] * (INV_ROOT / KEEP_RATE)).astype(target.dtype)
        target[:, E : 2 * E] = (sum_scr[rows, E : 2 * E] * (1.0 / KEEP_RATE)).astype(target.dtype)
        low += target.shape[0]


def attention(doc_ids, drop_bits, pieces, kv_parts, grads):
    slots, count, parts = len(grads), len(pieces), len(kv_parts)
    tokens, width = pieces[0].shape[0], grads[0].shape[1]
    heads = width // E
    blocks = sum(part.shape[0] for part in kv_parts) // BLK
    window = blocks - slots + 1
    body = functools.partial(
        attention_kernel,
        slots=slots,
        heads=heads,
        count=count,
        parts=parts,
    )
    outs = (
        [bf16(BLK, width)] * slots
        + [bf16(tokens, width)] * (count // 2)
        + [bf16(count // 2 * tokens, width)]
        + [jax.ShapeDtypeStruct(kv_parts[-1].shape, jnp.float32)]
        + [bf16(*part.shape) for part in kv_parts[:-1]]
    )
    results = kernel_call(
        body,
        outs,
        [VMEM] * (2 + count + parts + slots),
        [
            pltpu.VMEM((slots * heads * BLK, E), jnp.bfloat16),
            pltpu.VMEM((blocks * BLK, 2 * E), jnp.bfloat16),
            pltpu.VMEM((heads * BLK // WORD, BLK), jnp.int32),
            pltpu.VMEM((blocks, heads * BLK // WORD, BLK), jnp.int32),
            pltpu.VMEM((window * BLK, heads * BLK), jnp.bfloat16),
            pltpu.VMEM((window * BLK, heads * BLK), jnp.bfloat16),
            pltpu.VMEM((blocks * BLK, 2 * E), jnp.float32),
            pltpu.VMEM((slots * heads * BLK, E), jnp.bfloat16),
        ],
        flops=12 * slots * heads * window * BLK * BLK * E,
    )(doc_ids.reshape(1, -1), drop_bits.swapaxes(1, 2), *pieces, *kv_parts, *grads)
    out, results = results[:slots], results[slots:]
    near, far, results = results[: count // 2], results[count // 2], results[count // 2 + 1 :]
    return out, near, far, results[0], results[1:]


def swap(piece, m):
    return lax.ppermute(piece, "head", [(i, i ^ m) for i in range(lax.axis_size("head"))])


def exchange(pieces, places):
    return [swap(piece, m) if m in places else piece for m, piece in enumerate(pieces)]


def relay(mask, reach, block):
    count = lax.axis_size("ctx")
    return lax.ppermute(block, "ctx", [(i, i ^ mask) for i in range(count)]) if mask else block


def by_branch(branch, step, block, *operands):
    count = lax.axis_size("ctx")
    if count <= MOST_BRANCHES:
        branches = [functools.partial(step, m, reach) for m in range(count) for reach in (False, True)]
        return lax.switch(branch, branches, block, *operands)
    block = lax.switch(branch // 2, [functools.partial(relay, m, True) for m in range(count)], block)
    return step(0, True, block, *operands)


def on_device(query, key, value, grad_out, doc_ids, relay_mask, drop_bits):
    shards = lax.axis_size("ctx")
    count = lax.axis_size("head")
    slots, tokens = grad_out.shape[0] // BLK, key.shape[0]
    window = doc_ids.shape[0] // DOC_SHARE
    ahead = [(s, min(window - 1 - (s - 1) * slots, slots)) for s in range(1, -(-(window - 1) // slots) + 1)]

    def gather(mask, reach, grad, pieces):
        grad = relay(mask, reach, grad)
        kv, *tails = join(pieces, [sent * BLK for _, sent in ahead if sent < slots])
        parts = [kv]
        for s, sent in ahead:
            block = kv if sent == slots else tails.pop(0)
            if s < farthest or reach:
                block = lax.ppermute(block, "ctx", [(i, i + s) for i in range(shards - s)])
            parts.insert(0, block)
        return grad, parts

    def scatter(mask, reach, out, backs, near):
        out = relay(mask, reach, out)
        backs = [
            lax.ppermute(back, "ctx", [(i + s, i) for i in range(shards - s)]) if s < farthest or reach else back
            for (s, _), back in zip(ahead, reversed(backs))
        ]
        return out, backs, exchange(near, range(1, count // 2))

    def finish(mask, reach, out, first_out, own, backs, near, far):
        out = relay(mask, reach, out)
        passed = [far[m * tokens : (m + 1) * tokens] for m in range(count // 2)]
        passed = [swap(passed[m], m) for m in range(1, count // 2)]
        kv_grads = exchange(combine(own, backs, count), range(1, count))
        grad_q, whole = spread(first_out, [*near, *passed], far, slots)
        grad_k, grad_v = spread_kv(whole, kv_grads)
        return place(whole, out, 1), grad_q, grad_k, grad_v

    farthest = ahead[-1][0]
    gap = (farthest - 1) * slots + 1
    meets = (doc_ids[gap:] == doc_ids[:-gap]) & (jnp.arange(gap, doc_ids.shape[0]) % slots == 0)
    branches = jnp.max(2 * relay_mask[:, None] + meets.astype(jnp.int32)[None, :], axis=1)

    pieces, grads = pack(query, key, value, grad_out, count)
    pieces = exchange(pieces, range(1, count))
    grad_0 = by_branch(branches[0], relay, grads[0])
    grad_1, parts = by_branch(branches[1], gather, grads[1], pieces)
    out, near, far, own, backs = attention(doc_ids, drop_bits, pieces, parts, [grad_0, grad_1])
    far = swap(far, count // 2)
    out_0, backs, near = by_branch(branches[0], scatter, out[0], backs, near)
    return by_branch(branches[1], finish, out[1], out_0, own, backs, near, far)


def solution(mesh):
    placed = (
        P(("ctx", "head"), None),
        P(("ctx", "head"), None),
        P(("ctx", "head"), None),
        P("ctx", "head"),
        P(),
        P(),
        P("head", None, None),
    )
    return jax.shard_map(
        on_device,
        mesh=mesh,
        in_specs=placed,
        out_specs=(
            P("ctx", "head"),
            P(("ctx", "head"), None),
            P(("ctx", "head"), None),
            P(("ctx", "head"), None),
        ),
        check_vma=False,
    )
```

```python
import functools
import math

import jax
import jax.numpy as jnp
from jax import lax
from jax.experimental import pallas as pl
from jax.experimental.pallas import tpu as pltpu
from jax.sharding import PartitionSpec as P

E = 128
BLK = 128
WORD = 32

DOC_SHARE = 4

KEEP_RATE = 0.9
NEG = -1e30
INV_ROOT = 1.0 / math.sqrt(E)
LOG2 = INV_ROOT * math.log2(math.e)

MOST_BRANCHES = 8

VMEM_LIMIT = 48 * 1024 * 1024
PACK_LIMIT = 62 * 1024 * 1024

SMEM = pl.BlockSpec(memory_space=pltpu.SMEM)
VMEM = pl.BlockSpec(memory_space=pltpu.VMEM)
HBM = pl.BlockSpec(memory_space=pltpu.HBM)


def nt_dot(a, b):
    return lax.dot_general(a, b, (((1,), (1,)), ((), ())), preferred_element_type=jnp.float32)


def nn_dot(a, b):
    return lax.dot_general(a, b, (((1,), (0,)), ((), ())), preferred_element_type=jnp.float32)


def tn_dot(a, b):
    return lax.dot_general(a, b, (((0,), (0,)), ((), ())), preferred_element_type=jnp.float32)


def kernel_call(body, outs, specs, scratch=(), flops=0, touched=1 << 20):
    return pl.pallas_call(
        body,
        out_shape=outs,
        in_specs=specs,
        out_specs=jax.tree.map(lambda _: VMEM, outs),
        scratch_shapes=list(scratch),
        compiler_params=pltpu.CompilerParams(vmem_limit_bytes=VMEM_LIMIT),
        cost_estimate=pl.CostEstimate(flops=flops, bytes_accessed=touched, transcendentals=0),
    )


def bf16(*shape):
    return jax.ShapeDtypeStruct(shape, jnp.bfloat16)


def pack_kernel(query_ref, key_ref, value_ref, grad_ref, *refs, count, slots):
    results, (sems, result_sems, *out_refs) = refs[: count + slots], refs[count + slots :]
    piece_refs, grad_refs = out_refs[:count], out_refs[count:]
    width = query_ref.shape[1] // count
    copies = []
    for m in range(count):
        group = lax.axis_index("head") ^ m
        columns = pl.ds(pl.multiple_of(group * E, E), E)
        copies.append((key_ref.at[:, columns], piece_refs[m].at[:, 0:E]))
        copies.append((value_ref.at[:, columns], piece_refs[m].at[:, E : 2 * E]))
        columns = pl.ds(pl.multiple_of(group * width, E), width)
        copies.append((query_ref.at[:, columns], piece_refs[m].at[:, 2 * E :]))
    for slot in range(slots):
        copies.append((grad_ref.at[slot * BLK : (slot + 1) * BLK, :], grad_refs[slot]))
    started = [pltpu.make_async_copy(*pair, sems.at[i]) for i, pair in enumerate(copies)]
    for copy in started:
        copy.start()
    moved = [pltpu.make_async_copy(*pair, result_sems.at[i]) for i, pair in enumerate(zip(out_refs, results))]
    for m in range(count):
        for copy in started[3 * m : 3 * m + 3]:
            copy.wait()
        moved[m].start()
    for slot in range(slots):
        started[3 * count + slot].wait()
        moved[count + slot].start()
    for copy in moved:
        copy.wait()


def pack(query, key, value, grad, count):
    tokens, slots = key.shape[0], grad.shape[0] // BLK
    outs = [bf16(tokens, 2 * E + query.shape[1] // count)] * count + [bf16(BLK, grad.shape[1])] * slots
    pieces = pl.pallas_call(
        functools.partial(pack_kernel, count=count, slots=slots),
        out_shape=outs,
        in_specs=[HBM, HBM, HBM, HBM],
        out_specs=[HBM] * len(outs),
        scratch_shapes=[pltpu.SemaphoreType.DMA((3 * count + slots,)), pltpu.SemaphoreType.DMA((count + slots,))]
        + [pltpu.VMEM(out.shape, out.dtype) for out in outs],
        compiler_params=pltpu.CompilerParams(vmem_limit_bytes=PACK_LIMIT),
    )(query, key, value, grad)
    return pieces[:count], pieces[count:]


def join_kernel(*refs, count):
    piece_refs, (out_ref, *tail_refs) = refs[:count], refs[count:]
    tokens = piece_refs[0].shape[0]
    for m, piece in enumerate(piece_refs):
        start = pl.multiple_of((lax.axis_index("head") ^ m) * tokens, tokens)
        out_ref[pl.ds(start, tokens), :] = piece[:, 0 : 2 * E]
    for tail in tail_refs:
        tail[...] = out_ref[out_ref.shape[0] - tail.shape[0] :, :]


def join(pieces, lengths):
    rows, count = pieces[0].shape[0] * len(pieces), len(pieces)
    return kernel_call(
        functools.partial(join_kernel, count=count),
        [bf16(rows, 2 * E)] + [bf16(length, 2 * E) for length in lengths],
        [VMEM] * count,
    )(*pieces)


def spread_kernel(out_ref, *refs, count):
    piece_refs, (far_ref, query_ref, whole_ref, sem) = refs[: count - 1], refs[count - 1 :]
    tokens = query_ref.shape[0]
    copy = pltpu.make_async_copy(out_ref, whole_ref.at[0:BLK, :], sem)
    copy.start()
    width = query_ref.shape[1] // count
    places = [m for m in range(count) if m != count // 2]
    for m, piece in zip([*places, count // 2], [*piece_refs, far_ref.at[0:tokens, :]]):
        group = lax.axis_index("head") ^ m
        query_ref[:, pl.ds(pl.multiple_of(group * width, E), width)] = piece[...]
    copy.wait()


def spread(out, pieces, far, slots):
    count = len(pieces) + 1
    tokens, width = pieces[0].shape
    return pl.pallas_call(
        functools.partial(spread_kernel, count=count),
        out_shape=[bf16(tokens, count * width), bf16(slots * BLK, width)],
        in_specs=[VMEM] * (1 + count),
        out_specs=[VMEM, HBM],
        scratch_shapes=[pltpu.SemaphoreType.DMA],
        compiler_params=pltpu.CompilerParams(vmem_limit_bytes=VMEM_LIMIT),
    )(out, *pieces, far)


def spread_kv_kernel(after_ref, *refs, count):
    piece_refs, (key_ref, value_ref) = refs[:count], refs[count:]
    for m, piece in enumerate(piece_refs):
        columns = pl.ds(pl.multiple_of((lax.axis_index("head") ^ m) * E, E), E)
        key_ref[:, columns] = piece[:, 0:E]
        value_ref[:, columns] = piece[:, E : 2 * E]


def spread_kv(after, pieces):
    count = len(pieces)
    outs = [bf16(pieces[0].shape[0], count * E)] * 2
    return kernel_call(functools.partial(spread_kv_kernel, count=count), outs, [HBM] + [VMEM] * count)(
        after, *pieces
    )


def place_kernel(whole_ref, out_ref, placed_ref, sem, *, slot):
    copy = pltpu.make_async_copy(out_ref, placed_ref.at[slot * BLK : (slot + 1) * BLK, :], sem)
    copy.start()
    copy.wait()


def place(whole, out, slot):
    return pl.pallas_call(
        functools.partial(place_kernel, slot=slot),
        out_shape=bf16(*whole.shape),
        in_specs=[HBM, VMEM],
        out_specs=HBM,
        scratch_shapes=[pltpu.SemaphoreType.DMA],
        input_output_aliases={0: 0},
        compiler_params=pltpu.CompilerParams(vmem_limit_bytes=VMEM_LIMIT),
    )(whole, out)


def combine_kernel(own_ref, *refs, backs, count):
    back_refs, out_refs = refs[:backs], refs[backs:]
    rows = own_ref.shape[0]
    tokens = rows // count
    total = own_ref[...]
    for back in back_refs:
        term = back[...].astype(jnp.float32)
        if term.shape[0] < rows:
            term = jnp.concatenate([jnp.zeros((rows - term.shape[0], term.shape[1]), jnp.float32), term], 0)
        total = total + term
    own_ref[...] = total
    for m in range(count):
        start = pl.multiple_of((lax.axis_index("head") ^ m) * tokens, tokens)
        out_refs[m][...] = own_ref[pl.ds(start, tokens), :].astype(jnp.bfloat16)


def combine(own, backs, count):
    rows, width = own.shape

    def body(own_ref, *refs):
        *refs, total_ref = refs
        total_ref[...] = own_ref[...]
        combine_kernel(total_ref, *refs, backs=len(backs), count=count)

    return kernel_call(
        body,
        [bf16(rows // count, width)] * count,
        [VMEM] * (1 + len(backs)),
        [pltpu.VMEM(own.shape, jnp.float32)],
    )(own, *backs)


def attention_kernel(*refs, slots, heads, count, parts):
    (doc_ref, bits_ref), rest = refs[:2], refs[2:]
    query_refs, rest = rest[:count], rest[count:]
    part_refs, rest = rest[:parts], rest[parts:]
    grad_refs, rest = rest[:slots], rest[slots:]
    out_refs, rest = rest[:slots], rest[slots:]
    query_grad_refs, far_ref, rest = rest[: count // 2], rest[count // 2], rest[count // 2 + 1 :]
    own_ref, rest = rest[0], rest[1:]
    back_refs, rest = rest[: parts - 1], rest[parts - 1 :]
    query_scr, kv_scr, bits_scr, rolled_scr, weight_scr, dscore_scr, sum_scr, result_scr = rest
    blocks = kv_scr.shape[0] // BLK
    window = blocks - slots + 1
    first = lax.axis_index("ctx") * slots - (window - 1)
    tokens = query_refs[0].shape[0]
    per_block = BLK // tokens

    for m in range(count):
        owner = lax.axis_index("head") ^ m
        slot, place = owner // per_block, owner % per_block
        for h in range(heads):
            start = pl.multiple_of(slot * (heads * BLK) + h * BLK + place * tokens, tokens)
            query_scr[pl.ds(start, tokens), :] = query_refs[m][:, (h + 2) * E : (h + 3) * E]
    low = 0
    for part in part_refs:
        kv_scr[low : low + part.shape[0], :] = part[...]
        low += part.shape[0]

    words = BLK // WORD
    for h in range(heads):
        bits_scr[h * words : (h + 1) * words, :] = bits_ref[h]
    for w in range(blocks):
        rolled_scr[w] = pltpu.roll(bits_scr[...], (BLK - first - w) & (BLK - 1), axis=1)
    to_sign = WORD - 1 - lax.broadcasted_iota(jnp.int32, (WORD, BLK), 0)

    docs = doc_ref[...].astype(jnp.float32)
    numbers = lax.broadcasted_iota(jnp.int32, docs.shape, 1)
    for slot in range(slots):
        own = jnp.max(jnp.where(numbers == first + slot + window - 1, docs, NEG), axis=1, keepdims=True)
        biases = []
        for w in range(window - 1):
            document = jnp.max(jnp.where(numbers == first + slot + w, docs, NEG), axis=1, keepdims=True)
            biases.append(jnp.where(document == own, 0.0, NEG))
        rows = slice(slot * BLK, (slot + window) * BLK)
        queries = query_scr[slot * heads * BLK : (slot + 1) * heads * BLK, :]
        grads = jnp.concatenate([grad_refs[slot][:, h * E : (h + 1) * E] for h in range(heads)], axis=0)
        keys, values = kv_scr[rows, 0:E], kv_scr[rows, E : 2 * E]

        def head_step(h, _, slot=slot, biases=biases):
            cols = pl.ds(pl.multiple_of(h * BLK, BLK), BLK)
            causal = lax.broadcasted_iota(jnp.int32, (BLK, BLK), 0) <= lax.broadcasted_iota(
                jnp.int32, (BLK, BLK), 1
            )
            tiles = []
            own_queries = query_scr[pl.ds(pl.multiple_of((slot * heads + h) * BLK, BLK), BLK), :]
            scores = nt_dot(keys, own_queries)
            own_grads = grad_refs[slot][:, cols]
            dweights = nt_dot(values, own_grads)
            for w in range(window):
                tile = scores[w * BLK : (w + 1) * BLK]
                tiles.append(jnp.where(causal, tile, NEG) if w == window - 1 else tile)
            tops = [jnp.max(tile, axis=0, keepdims=True) for tile in tiles]
            offsets = [*biases, jnp.zeros_like(tops[-1])]
            top = functools.reduce(jnp.maximum, [a + b for a, b in zip(tops, offsets)])
            probs = [jnp.exp2((tile - (top - b)) * LOG2) for tile, b in zip(tiles, offsets)]
            scale = 1.0 / jnp.sum(functools.reduce(jnp.add, probs), axis=0, keepdims=True)
            delta = jnp.zeros((BLK, BLK), jnp.float32)
            kept = []
            for w in range(window):
                block = slice(w * BLK, (w + 1) * BLK)
                keep = [
                    jnp.left_shift(
                        jnp.broadcast_to(rolled_scr[slot + w, pl.ds(h * words + q, 1), :], (WORD, BLK)), to_sign
                    )
                    for q in range(words)
                ]
                keep = jnp.concatenate(keep, axis=0) < 0
                probs[w] = probs[w] * scale
                weight = jnp.where(keep, probs[w], 0.0)
                weight_scr[block, cols] = weight.astype(jnp.bfloat16)
                kept.append(weight * dweights[w * BLK : (w + 1) * BLK])
                delta = delta + kept[w]
            delta = jnp.sum(delta, axis=0, keepdims=True)
            for w in range(window):
                dscore_scr[w * BLK : (w + 1) * BLK, cols] = (kept[w] - probs[w] * delta).astype(jnp.bfloat16)
            return 0

        lax.fori_loop(0, heads, head_step, 0, unroll=8)
        out = tn_dot(values, weight_scr[...])
        query_grad = tn_dot(keys, dscore_scr[...])
        for h in range(heads):
            cols = slice(h * BLK, (h + 1) * BLK)
            out_refs[slot][:, h * E : (h + 1) * E] = (out[:, cols].T * (1.0 / KEEP_RATE)).astype(jnp.bfloat16)
            start = (slot * heads + h) * BLK
            result_scr[start : start + BLK, :] = (query_grad[:, cols].T * (INV_ROOT / KEEP_RATE)).astype(
                jnp.bfloat16
            )
        if slot == 0:
            sum_scr[window * BLK :, :] = jnp.zeros_like(sum_scr[window * BLK :, :])
            sum_scr[rows, 0:E] = nn_dot(dscore_scr[...], queries)
            sum_scr[rows, E : 2 * E] = nn_dot(weight_scr[...], grads)
        else:
            sum_scr[rows, 0:E] += nn_dot(dscore_scr[...], queries)
            sum_scr[rows, E : 2 * E] += nn_dot(weight_scr[...], grads)

    for m in range(count):
        owner = lax.axis_index("head") ^ m
        slot, place = owner // per_block, owner % per_block
        for h in range(heads):
            start = pl.multiple_of(slot * (heads * BLK) + h * BLK + place * tokens, tokens)
            piece = result_scr[pl.ds(start, tokens), :]
            if m < count // 2:
                query_grad_refs[m][:, h * E : (h + 1) * E] = piece
            else:
                far_ref[(m - count // 2) * tokens : (m + 1 - count // 2) * tokens, h * E : (h + 1) * E] = piece
    low = 0
    for target in (*back_refs, own_ref):
        rows = slice(low, low + target.shape[0])
        target[:, 0:E] = (sum_scr[rows, 0:E] * (INV_ROOT / KEEP_RATE)).astype(target.dtype)
        target[:, E : 2 * E] = (sum_scr[rows, E : 2 * E] * (1.0 / KEEP_RATE)).astype(target.dtype)
        low += target.shape[0]


def attention(doc_ids, drop_bits, pieces, kv_parts, grads):
    slots, count, parts = len(grads), len(pieces), len(kv_parts)
    tokens, width = pieces[0].shape[0], grads[0].shape[1]
    heads = width // E
    blocks = sum(part.shape[0] for part in kv_parts) // BLK
    window = blocks - slots + 1
    body = functools.partial(
        attention_kernel,
        slots=slots,
        heads=heads,
        count=count,
        parts=parts,
    )
    outs = (
        [bf16(BLK, width)] * slots
        + [bf16(tokens, width)] * (count // 2)
        + [bf16(count // 2 * tokens, width)]
        + [jax.ShapeDtypeStruct(kv_parts[-1].shape, jnp.float32)]
        + [bf16(*part.shape) for part in kv_parts[:-1]]
    )
    results = kernel_call(
        body,
        outs,
        [VMEM] * (2 + count + parts + slots),
        [
            pltpu.VMEM((slots * heads * BLK, E), jnp.bfloat16),
            pltpu.VMEM((blocks * BLK, 2 * E), jnp.bfloat16),
            pltpu.VMEM((heads * BLK // WORD, BLK), jnp.int32),
            pltpu.VMEM((blocks, heads * BLK // WORD, BLK), jnp.int32),
            pltpu.VMEM((window * BLK, heads * BLK), jnp.bfloat16),
            pltpu.VMEM((window * BLK, heads * BLK), jnp.bfloat16),
            pltpu.VMEM((blocks * BLK, 2 * E), jnp.float32),
            pltpu.VMEM((slots * heads * BLK, E), jnp.bfloat16),
        ],
        flops=12 * slots * heads * window * BLK * BLK * E,
    )(doc_ids.reshape(1, -1), drop_bits.swapaxes(1, 2), *pieces, *kv_parts, *grads)
    out, results = results[:slots], results[slots:]
    near, far, results = results[: count // 2], results[count // 2], results[count // 2 + 1 :]
    return out, near, far, results[0], results[1:]


def swap(piece, m):
    return lax.ppermute(piece, "head", [(i, i ^ m) for i in range(lax.axis_size("head"))])


def exchange(pieces, places):
    return [swap(piece, m) if m in places else piece for m, piece in enumerate(pieces)]


def relay(mask, reach, block):
    count = lax.axis_size("ctx")
    return lax.ppermute(block, "ctx", [(i, i ^ mask) for i in range(count)]) if mask else block


def by_branch(branch, step, block, *operands):
    count = lax.axis_size("ctx")
    if count <= MOST_BRANCHES:
        branches = [functools.partial(step, m, reach) for m in range(count) for reach in (False, True)]
        return lax.switch(branch, branches, block, *operands)
    block = lax.switch(branch // 2, [functools.partial(relay, m, True) for m in range(count)], block)
    return step(0, True, block, *operands)


def on_device(query, key, value, grad_out, doc_ids, relay_mask, drop_bits):
    shards = lax.axis_size("ctx")
    count = lax.axis_size("head")
    slots, tokens = grad_out.shape[0] // BLK, key.shape[0]
    window = doc_ids.shape[0] // DOC_SHARE
    ahead = [(s, min(window - 1 - (s - 1) * slots, slots)) for s in range(1, -(-(window - 1) // slots) + 1)]

    def gather(mask, reach, grad, pieces):
        grad = relay(mask, reach, grad)
        kv, *tails = join(pieces, [sent * BLK for _, sent in ahead if sent < slots])
        parts = [kv]
        for s, sent in ahead:
            block = kv if sent == slots else tails.pop(0)
            if s < farthest or reach:
                block = lax.ppermute(block, "ctx", [(i, i + s) for i in range(shards - s)])
            parts.insert(0, block)
        return grad, parts

    def scatter(mask, reach, out, backs, near):
        out = relay(mask, reach, out)
        backs = [
            lax.ppermute(back, "ctx", [(i + s, i) for i in range(shards - s)]) if s < farthest or reach else back
            for (s, _), back in zip(ahead, reversed(backs))
        ]
        return out, backs, exchange(near, range(1, count // 2))

    def finish(mask, reach, out, first_out, own, backs, near, far):
        out = relay(mask, reach, out)
        passed = [far[m * tokens : (m + 1) * tokens] for m in range(count // 2)]
        passed = [swap(passed[m], m) for m in range(1, count // 2)]
        kv_grads = exchange(combine(own, backs, count), range(1, count))
        grad_q, whole = spread(first_out, [*near, *passed], far, slots)
        grad_k, grad_v = spread_kv(whole, kv_grads)
        return place(whole, out, 1), grad_q, grad_k, grad_v

    farthest = ahead[-1][0]
    gap = (farthest - 1) * slots + 1
    meets = (doc_ids[gap:] == doc_ids[:-gap]) & (jnp.arange(gap, doc_ids.shape[0]) % slots == 0)
    branches = jnp.max(2 * relay_mask[:, None] + meets.astype(jnp.int32)[None, :], axis=1)

    pieces, grads = pack(query, key, value, grad_out, count)
    pieces = exchange(pieces, range(1, count))
    grad_0 = by_branch(branches[0], relay, grads[0])
    grad_1, parts = by_branch(branches[1], gather, grads[1], pieces)
    out, near, far, own, backs = attention(doc_ids, drop_bits, pieces, parts, [grad_0, grad_1])
    far = swap(far, count // 2)
    out_0, backs, near = by_branch(branches[0], scatter, out[0], backs, near)
    return by_branch(branches[1], finish, out[1], out_0, own, backs, near, far)


def solution(mesh):
    placed = (
        P(("ctx", "head"), None),
        P(("ctx", "head"), None),
        P(("ctx", "head"), None),
        P("ctx", "head"),
        P(),
        P(),
        P("head", None, None),
    )
    return jax.shard_map(
        on_device,
        mesh=mesh,
        in_specs=placed,
        out_specs=(
            P("ctx", "head"),
            P(("ctx", "head"), None),
            P(("ctx", "head"), None),
            P(("ctx", "head"), None),
        ),
        check_vma=False,
    )
```
